32 devices in a mesh: space: 8 (over y, x, core), chan: 4 (over z).
Axes of the slice: x: 2, y: 2, z: 4, core: 2. Of those that a mesh axis runs over, the one named last changes fastest.
Arguments:
- images: bfloat16 [768, 64, 256], P('chan', 'space'), may hold values from -6 to 6
- weight: bfloat16 [3, 3, 768, 768], P(None, None, 'chan'), may hold values from -0.078125 to 0.078125
- cotangent: bfloat16 [768, 64, 256], P('chan', 'space'), may hold values from -6 to 6
Outputs:
- activated: bfloat16 [768, 64, 256], P('chan', 'space')
- input_grad: bfloat16 [768, 64, 256], P('chan', 'space')
- weight_grad: float32 [3, 3, 768, 768], P(None, None, 'chan')
The draws below stay inside these ranges and needn't reach their ends.
All inputs are finite; a program needn't handle non-finite values.
Results may differ from the reference program's by a relative error of at most 0.005.
Values may be sent and summed in bfloat16 or wider, within the bound.
A program may use at most 128 MiB of HBM per device.

```python
import jax
import jax.numpy as jnp

C = 768
WIDTH = 256
H = 64


def steps_of(key, dims, pieces, low, top_value):
    factor_of, own = 1.0, jax.random.fold_in(key, 6)
    for dim, blocks in pieces:
        heights = jnp.exp(jax.random.uniform(jax.random.fold_in(own, dim), (blocks,), jnp.float32, low / len(pieces), top_value / len(pieces)))
        factor_of = factor_of * jnp.repeat(heights, dims[dim] // blocks).reshape([-1 if axis == dim else 1 for axis in range(len(dims))])
    return factor_of


def bell_draw(stream_key, extent, spread, bound, split=(), held_as=jnp.bfloat16):
    values = jax.random.normal(stream_key, extent, jnp.float32) * spread
    if len(split) > 0:
        values = steps_of(stream_key, extent, split, -0.22, 0.18) * values
    return jnp.clip(values, min=-bound, max=bound).astype(held_as)


def setup_inputs(seed: int = 0) -> dict:
    keys = jax.random.split(jax.random.key(seed), 4)
    images = bell_draw(keys[0], (C, H, WIDTH), 1.0, 6.0, ((0, 4), (1, 8)))
    weight = bell_draw(keys[1], (3, 3, C, C), (9 * C) ** -0.5, 0.078125, ((2, 4),))
    cotangent = bell_draw(keys[2], (C, H, WIDTH), 1.0, 6.0, ((0, 4), (1, 8)))
    return {"images": images, "weight": weight, "cotangent": cotangent}


def reference(images, weight, cotangent):
    rows = images.shape[1]
    width = images.shape[2]
    padded = jnp.pad(images, ((0, 0), (1, 1), (1, 1))).astype(jnp.float32)
    kernel = weight.astype(jnp.float32)
    pre = jnp.zeros((weight.shape[2], rows, width), jnp.float32)
    for row_tap in range(3):
        for col_tap in range(3):
            pre = pre + jnp.einsum('oi,ihw->ohw', kernel[row_tap, col_tap], padded[:, row_tap:row_tap + rows, col_tap:col_tap + width])
    sigma = jax.nn.sigmoid(pre)
    activated = (pre * sigma).astype(jnp.bfloat16)
    pre_grad = (cotangent.astype(jnp.float32) * sigma * (1.0 + pre * (1.0 - sigma))).astype(jnp.bfloat16)
    grad_pad = jnp.pad(pre_grad, ((0, 0), (1, 1), (1, 1))).astype(jnp.float32)
    gradient = pre_grad.astype(jnp.float32)
    input_grad = jnp.zeros((weight.shape[3], rows, width), jnp.float32)
    taps = []
    for row_tap in range(3):
        line = []
        for col_tap in range(3):
            input_grad = input_grad + jnp.einsum('oi,ohw->ihw', kernel[row_tap, col_tap], grad_pad[:, 2 - row_tap:2 - row_tap + rows, 2 - col_tap:2 - col_tap + width])
            line.append(jnp.einsum('ihw,ohw->oi', padded[:, row_tap:row_tap + rows, col_tap:col_tap + width], gradient))
        taps.append(jnp.stack(line))
    weight_grad = jnp.stack(taps)
    return activated, input_grad.astype(jnp.bfloat16), weight_grad
```

```python
import jax
import jax.numpy as jnp
from jax import lax
from jax.sharding import PartitionSpec as P


def with_halo(array, sides, width):
    for axis, dim in sides:
        peers, length = (lax.axis_size(axis), array.shape[dim])
        up = [(i, (i + 1) % peers) for i in range(peers - 1)]
        down = [(j, i) for i, j in up]
        last = lax.slice_in_dim(array, length - width, length, axis=dim)
        leading = lax.slice_in_dim(array, 0, width, axis=dim)
        before = lax.ppermute(last, axis, up)
        after = lax.ppermute(leading, axis, down)
        array = jnp.concatenate([before, array, after], axis=dim)
    return array


def widen(block):
    return jnp.pad(block, ((0, 0), (0, 0), (1, 1)))


def forward_add(total, piece, weight):
    rows = total.shape[1]
    width = total.shape[2]
    wide = widen(piece)
    for row_tap in range(3):
        for col_tap in range(3):
            total = total + jnp.einsum(
                "oi,ihw->ohw",
                weight[row_tap, col_tap],
                wide[:, row_tap : row_tap + rows, col_tap : col_tap + width],
                preferred_element_type=jnp.float32,
            )
    return total


def wgrad_add(piece, gradient):
    rows = gradient.shape[1]
    width = gradient.shape[2]
    wide = widen(piece)
    taps = []
    for row_tap in range(3):
        line = []
        for col_tap in range(3):
            line.append(
                jnp.einsum(
                    "ihw,ohw->oi",
                    wide[:, row_tap : row_tap + rows, col_tap : col_tap + width],
                    gradient,
                    preferred_element_type=jnp.float32,
                )
            )
        taps.append(jnp.stack(line))
    terms = jnp.stack(taps)
    return terms


def transpose_taps(kernel, wide, rows, width):
    total = None
    for row_tap in range(3):
        for col_tap in range(3):
            term = jnp.einsum(
                "oi,ohw->ihw",
                kernel[row_tap, col_tap],
                wide[:, 2 - row_tap : 2 - row_tap + rows, 2 - col_tap : 2 - col_tap + width],
                preferred_element_type=jnp.float32,
            )
            total = term if total is None else total + term
    return total


def on_device(images, weight, cotangent):
    block = images.shape[0]
    rows = images.shape[1]
    width = images.shape[2]
    gathered = lax.all_gather(images, "chan", axis=0, tiled=True)
    framed = with_halo(gathered, (("space", 1),), 1)
    empty = jnp.zeros((block, rows, width), jnp.float32)
    pre = forward_add(empty, framed, weight)
    sigma = jax.nn.sigmoid(pre)
    activated = (pre * sigma).astype(jnp.bfloat16)
    pre_grad = (cotangent.astype(jnp.float32) * sigma * (1.0 + pre * (1.0 - sigma))).astype(
        jnp.bfloat16
    )
    grad_framed = with_halo(pre_grad, (("space", 1),), 1)
    grad_wide = widen(grad_framed)
    partial = transpose_taps(weight, grad_wide, rows, width).astype(jnp.bfloat16)
    input_grad = lax.psum_scatter(partial, "chan", scatter_dimension=0, tiled=True)
    local_wgrad = wgrad_add(framed, pre_grad).astype(jnp.bfloat16)
    weight_grad = lax.psum(local_wgrad, "space").astype(jnp.float32)
    return (activated, input_grad, weight_grad)


def solution(mesh):
    return jax.shard_map(
        on_device,
        mesh=mesh,
        in_specs=(P("chan", "space", None), P(None, None, "chan", None), P("chan", "space", None)),
        out_specs=(P("chan", "space", None), P("chan", "space", None), P(None, None, "chan", None)),
        check_vma=False,
    )
```

```python
import functools

import jax
import jax.numpy as jnp
from jax import lax
from jax.experimental import pallas as pl
from jax.experimental.pallas import tpu as pltpu
from jax.sharding import PartitionSpec as P

BF = jnp.bfloat16
F32 = jnp.float32
MESH = pl.DeviceIdType.MESH
CHUNKS = 2


def shifted(value, by):
    width = value.shape[1]
    col = lax.broadcasted_iota(jnp.int32, value.shape, 1)
    edge = width - 1 if by == 1 else 0
    return jnp.where(col == edge, 0.0, pltpu.roll(value, (-by) % width, 1))


def kernel(
    n, S, x_ref, ct_ref, wb_ref, wt_ref, act_ref, ig_ref, wg_ref,
    frame, acc, grads, sbuf, rbuf, part, pair_buf, chip_buf,
    own_sem, gs_sem, gr_sem, hs_sem, hr_sem, es_sem, er_sem, rs_sem, rr_sem,
    ps_sem, pr_sem, cs_sem, cr_sem, as_sem, ar_sem, fs_sem, fr_sem,
):
    R, Cb, W = x_ref.shape
    O = ct_ref.shape[1]
    T = 3 * O
    G = S // 2
    half = R // CHUNKS
    s = lax.axis_index("space")
    c = lax.axis_index("chan")

    barrier = pltpu.get_barrier_semaphore()
    for k in range(1, S):
        pl.semaphore_signal(barrier, 1, device_id=(lax.rem(s + k, S), c), device_id_type=MESH)

    @pl.when(c > 0)
    def _():
        pl.semaphore_signal(barrier, 1, device_id=(s, c - 1), device_id_type=MESH)

    @pl.when(c < n - 1)
    def _():
        pl.semaphore_signal(barrier, 1, device_id=(s, c + 1), device_id_type=MESH)

    own = pltpu.make_async_copy(x_ref, frame.at[c, pl.ds(1, R)], own_sem)
    own.start()
    zero_row = jnp.zeros((Cb, W), BF)

    @pl.when(s == 0)
    def _():
        for j in range(n):
            frame[j, 0] = zero_row
        grads[0] = jnp.zeros((T, W), BF)

    @pl.when(s == S - 1)
    def _():
        for j in range(n):
            frame[j, R + 1] = zero_row
        grads[R + 1] = jnp.zeros((T, W), BF)

    acc[...] = jnp.zeros_like(acc)
    pl.semaphore_wait(barrier, S - 1 + jnp.minimum(c, 1) + jnp.minimum(n - 1 - c, 1))
    own.wait()

    def peer(way):
        return (s, c + 1) if way == 0 else (s, c - 1)

    def gather_copy(way, step, part_no, block):
        rows = pl.ds(1 + part_no * half, half)
        return pltpu.make_async_remote_copy(
            src_ref=frame.at[block, rows], dst_ref=frame.at[block, rows],
            send_sem=gs_sem.at[way, step, part_no], recv_sem=gr_sem.at[way, step, part_no],
            device_id=peer(way), device_id_type=MESH,
        )

    def sends(way, step):
        if way == 0:
            return c - step, jnp.logical_and(c - step >= 0, c < n - 1)
        return c + step, jnp.logical_and(c + step <= n - 1, c > 0)

    def receives(way, step):
        if way == 0:
            return c - 1 - step, c - 1 - step >= 0
        return c + 1 + step, c + 1 + step <= n - 1

    def halo_copy(slot, side, block):
        src, dst, to = (R, 0, s + 1) if side == 0 else (1, R + 1, s - 1)
        return pltpu.make_async_remote_copy(
            src_ref=frame.at[block, src], dst_ref=frame.at[block, dst],
            send_sem=hs_sem.at[slot, side], recv_sem=hr_sem.at[slot, side],
            device_id=(to, c), device_id_type=MESH,
        )

    def halo_start(slot, block):
        @pl.when(s < S - 1)
        def _():
            halo_copy(slot, 0, block).start()

        @pl.when(s > 0)
        def _():
            halo_copy(slot, 1, block).start()

    def halo_wait(slot, block):
        @pl.when(s < S - 1)
        def _():
            halo_copy(slot, 0, block).wait_send()
            halo_copy(slot, 1, block).wait_recv()

        @pl.when(s > 0)
        def _():
            halo_copy(slot, 1, block).wait_send()
            halo_copy(slot, 0, block).wait_recv()

    def forward(block):
        def row(h, carry):
            total = acc[h]
            for a in range(3):
                total = total + jnp.dot(wb_ref[block, a], frame[block, h + a], preferred_element_type=F32)
            acc[h] = total
            return carry

        lax.fori_loop(0, R, row, 0)

    def start_gather(step, part_no):
        for way in range(2):
            block, valid = sends(way, step)

            @pl.when(valid)
            def _():
                gather_copy(way, step, part_no, block).start()

    for p in range(CHUNKS):
        start_gather(0, p)
    halo_start(0, c)
    halo_wait(0, c)
    forward(c)
    for step in range(n - 1):
        for p in range(CHUNKS):
            for way in range(2):
                block, valid = receives(way, step)

                @pl.when(valid)
                def _():
                    gather_copy(way, step, p, block).wait_recv()

            if step < n - 2:
                start_gather(step + 1, p)
        for way in range(2):
            block, valid = receives(way, step)

            @pl.when(valid)
            def _():
                halo_start(1 + 2 * step + way, block)
        for way in range(2):
            block, valid = receives(way, step)

            @pl.when(valid)
            def _():
                halo_wait(1 + 2 * step + way, block)
                forward(block)

    def activate(h):
        pre = shifted(acc[h, :O], -1) + acc[h, O : 2 * O] + shifted(acc[h, 2 * O :], 1)
        sigma = jax.nn.sigmoid(pre)
        act_ref[h] = (pre * sigma).astype(BF)
        grad = (ct_ref[h].astype(F32) * sigma * (1.0 + pre * (1.0 - sigma))).astype(BF)
        wide = grad.astype(F32)
        grads[h + 1, :O] = shifted(wide, 1).astype(BF)
        grads[h + 1, O : 2 * O] = grad
        grads[h + 1, 2 * O :] = shifted(wide, -1).astype(BF)

    def edge_copy(side):
        src, dst, to = (R, 0, s + 1) if side == 0 else (1, R + 1, s - 1)
        return pltpu.make_async_remote_copy(
            src_ref=grads.at[src], dst_ref=grads.at[dst],
            send_sem=es_sem.at[side], recv_sem=er_sem.at[side],
            device_id=(to, c), device_id_type=MESH,
        )

    def edges(k, carry):
        activate(k * (R - 1))
        return carry

    lax.fori_loop(0, 2, edges, 0)

    @pl.when(s < S - 1)
    def _():
        edge_copy(0).start()

    @pl.when(s > 0)
    def _():
        edge_copy(1).start()

    def middle(h, carry):
        activate(h)
        return carry

    lax.fori_loop(1, R - 1, middle, 0)

    @pl.when(s < S - 1)
    def _():
        edge_copy(0).wait_send()
        edge_copy(1).wait_recv()

    @pl.when(s > 0)
    def _():
        edge_copy(1).wait_send()
        edge_copy(0).wait_recv()

    def own_row(block, h):
        total = jnp.dot(wt_ref[block, 0], grads[h + 2], preferred_element_type=F32)
        total = total + jnp.dot(wt_ref[block, 1], grads[h + 1], preferred_element_type=F32)
        return total + jnp.dot(wt_ref[block, 2], grads[h], preferred_element_type=F32)

    def scatter_dest(way, step):
        far = n - 1 - step
        if way == 0:
            return c + far, c + far <= n - 1
        return c - far, c - far >= 0

    def scatter_arrives(way, step):
        far = n - 1 - step
        if way == 0:
            return jnp.logical_and(c >= 1, c - 1 + far <= n - 1)
        return jnp.logical_and(c <= n - 2, c + 1 - far >= 0)

    def scatter_copy(way, step, part_no):
        rows = pl.ds(part_no * half, half)
        return pltpu.make_async_remote_copy(
            src_ref=sbuf.at[way, step, rows], dst_ref=rbuf.at[way, step, rows],
            send_sem=rs_sem.at[way, step, part_no], recv_sem=rr_sem.at[way, step, part_no],
            device_id=peer(way), device_id_type=MESH,
        )

    def scatter_own(step, part_no):
        for way in range(2):
            dest, valid = scatter_dest(way, step)

            @pl.when(valid)
            def _():
                def row(h, carry):
                    sbuf[way, step, h] = own_row(dest, h).astype(BF)
                    return carry

                lax.fori_loop(part_no * half, (part_no + 1) * half, row, 0)

    def scatter_send(step, part_no):
        for way in range(2):
            _, valid = scatter_dest(way, step)
            if step > 0:
                arrived = scatter_arrives(way, step - 1)

                @pl.when(arrived)
                def _():
                    scatter_copy(way, step - 1, part_no).wait_recv()

                    def row(h, carry):
                        total = sbuf[way, step, h].astype(F32) + rbuf[way, step - 1, h].astype(F32)
                        sbuf[way, step, h] = total.astype(BF)
                        return carry

                    lax.fori_loop(part_no * half, (part_no + 1) * half, row, 0)

            @pl.when(valid)
            def _():
                scatter_copy(way, step, part_no).start()

    def wgrad(block):
        def tap(a, carry):
            total = jnp.zeros((T, Cb), F32)
            for h in range(R):
                total = total + lax.dot_general(
                    grads[h + 1], frame[block, h + a], (((1,), (1,)), ((), ())),
                    preferred_element_type=F32,
                )
            start = pl.multiple_of((block * 3 + a) * T, 16)
            part[pl.ds(start, T)] = total.astype(BF)
            return carry

        lax.fori_loop(0, 3, tap, 0)

    rows_all = part.shape[0]
    rows_half = rows_all // 2
    piece = rows_half // G
    side = lax.rem(s, 2)
    chip = lax.div(s, 2)
    mate = (s + 1 - 2 * side, c)
    mine = side * rows_half
    theirs = (1 - side) * rows_half

    def span(start, size):
        return pl.ds(pl.multiple_of(start, 16), size)

    def pair_copy():
        return pltpu.make_async_remote_copy(
            src_ref=part.at[span(theirs, rows_half)], dst_ref=pair_buf,
            send_sem=ps_sem, recv_sem=pr_sem, device_id=mate, device_id_type=MESH,
        )

    def chip_copy(k):
        to = lax.rem(chip + k, G)
        return pltpu.make_async_remote_copy(
            src_ref=part.at[span(mine + to * piece, piece)], dst_ref=chip_buf.at[k - 1],
            send_sem=cs_sem.at[k - 1], recv_sem=cr_sem.at[k - 1],
            device_id=(2 * to + side, c), device_id_type=MESH,
        )

    def share_copy(k):
        to = lax.rem(chip + k, G)
        rows = span(mine + chip * piece, piece)
        return pltpu.make_async_remote_copy(
            src_ref=wg_ref.at[rows], dst_ref=wg_ref.at[rows],
            send_sem=as_sem.at[k - 1], recv_sem=ar_sem.at[k - 1],
            device_id=(2 * to + side, c), device_id_type=MESH,
        )

    def mate_copy(k):
        origin = lax.rem(chip - k + G, G)
        rows = span(mine + origin * piece, piece)
        return pltpu.make_async_remote_copy(
            src_ref=wg_ref.at[rows], dst_ref=wg_ref.at[rows],
            send_sem=fs_sem.at[k], recv_sem=fr_sem.at[k],
            device_id=mate, device_id_type=MESH,
        )

    def reduce_stage(stage):
        if stage == 0:
            pair_copy().start()
        elif stage == 1:
            pair_copy().wait()

            def add(i, carry):
                rows = span(mine + i * 16, 16)
                got = pair_buf[span(i * 16, 16)].astype(F32)
                part[rows] = (part[rows].astype(F32) + got).astype(BF)
                return carry

            lax.fori_loop(0, rows_half // 16, add, 0, unroll=6)
            for k in range(1, G):
                chip_copy(k).start()
        elif stage == 2:
            for k in range(1, G):
                chip_copy(k).wait()

            def add(i, carry):
                rows = span(mine + chip * piece + i * 16, 16)
                total = part[rows].astype(F32)
                for k in range(1, G):
                    total = total + chip_buf[k - 1, span(i * 16, 16)].astype(F32)
                wg_ref[rows] = total.astype(BF)
                return carry

            lax.fori_loop(0, piece // 16, add, 0, unroll=3)
            for k in range(1, G):
                share_copy(k).start()
            mate_copy(0).start()
        else:
            for k in range(1, G):
                share_copy(k).wait()
                mate_copy(k).start()

    for p in range(CHUNKS):
        scatter_own(0, p)
        scatter_send(0, p)

    def all_wgrad(block, carry):
        wgrad(block)
        return carry

    lax.fori_loop(0, n, all_wgrad, 0)
    reduce_stage(0)
    stage = 1
    for step in range(1, n):
        if step < n - 1:
            for p in range(CHUNKS):
                scatter_own(step, p)
            if stage < 2:
                reduce_stage(stage)
                stage += 1
            for p in range(CHUNKS):
                scatter_send(step, p)
        else:
            def row(h, carry):
                acc[h, :Cb] = own_row(c, h)
                return carry

            lax.fori_loop(0, R, row, 0)
    while stage < 4:
        reduce_stage(stage)
        stage += 1

    for way in range(2):
        arrived = scatter_arrives(way, n - 2)

        @pl.when(arrived)
        def _():
            for p in range(CHUNKS):
                scatter_copy(way, n - 2, p).wait_recv()

            def row(h, carry):
                acc[h, :Cb] = acc[h, :Cb] + rbuf[way, n - 2, h].astype(F32)
                return carry

            lax.fori_loop(0, R, row, 0)

    def last(h, carry):
        ig_ref[h] = acc[h, :Cb].astype(BF)
        return carry

    lax.fori_loop(0, R, last, 0)

    for k in range(G):
        mate_copy(k).wait()
    for step in range(n - 1):
        for way in range(2):
            block, valid = sends(way, step)
            _, out = scatter_dest(way, step)

            @pl.when(valid)
            def _():
                for p in range(CHUNKS):
                    gather_copy(way, step, p, block).wait_send()

            @pl.when(out)
            def _():
                for p in range(CHUNKS):
                    scatter_copy(way, step, p).wait_send()


def on_device(n, S, images, weight, cotangent):
    Cb, R, W = images.shape
    O = weight.shape[2]
    T = 3 * O
    x = images.transpose(1, 0, 2)
    ct = cotangent.transpose(1, 0, 2)
    w = weight.reshape(3, 3, O, n, Cb)
    wb = w.transpose(3, 0, 1, 2, 4).reshape(n, 3, T, Cb)
    wt = w.transpose(3, 0, 4, 1, 2).reshape(n, 3, Cb, T)
    rows_all = n * 3 * T
    dma = pltpu.SemaphoreType.DMA
    vmem = pl.BlockSpec(memory_space=pltpu.VMEM)
    act, ig, wg = pl.pallas_call(
        functools.partial(kernel, n, S),
        out_shape=(
            jax.ShapeDtypeStruct((R, O, W), BF),
            jax.ShapeDtypeStruct((R, Cb, W), BF),
            jax.ShapeDtypeStruct((rows_all, Cb), BF),
        ),
        in_specs=[vmem] * 4,
        out_specs=(vmem, vmem, vmem),
        scratch_shapes=[
            pltpu.VMEM((n, R + 2, Cb, W), BF),
            pltpu.VMEM((R, T, W), F32),
            pltpu.VMEM((R + 2, T, W), BF),
            pltpu.VMEM((2, n - 1, R, Cb, W), BF),
            pltpu.VMEM((2, n - 1, R, Cb, W), BF),
            pltpu.VMEM((rows_all, Cb), BF),
            pltpu.VMEM((rows_all // 2, Cb), BF),
            pltpu.VMEM((S // 2 - 1, rows_all // S, Cb), BF),
            dma,
            dma((2, n - 1, CHUNKS)), dma((2, n - 1, CHUNKS)),
            dma((2 * n - 1, 2)), dma((2 * n - 1, 2)),
            dma((2,)), dma((2,)),
            dma((2, n - 1, CHUNKS)), dma((2, n - 1, CHUNKS)),
            dma, dma,
            dma((S // 2 - 1,)), dma((S // 2 - 1,)),
            dma((S // 2 - 1,)), dma((S // 2 - 1,)),
            dma((S // 2,)), dma((S // 2,)),
        ],
        compiler_params=pltpu.CompilerParams(
            collective_id=0, has_side_effects=True, vmem_limit_bytes=60 * 2**20
        ),
    )(x, ct, wb, wt)
    weight_grad = wg.astype(F32).reshape(n, 3, 3, O, Cb).transpose(1, 2, 3, 0, 4)
    return (
        act.transpose(1, 0, 2),
        ig.transpose(1, 0, 2),
        weight_grad.reshape(3, 3, O, n * Cb),
    )


def solution(mesh):
    return jax.shard_map(
        functools.partial(on_device, mesh.shape["chan"], mesh.shape["space"]),
        mesh=mesh,
        in_specs=(P("chan", "space", None), P(None, None, "chan", None), P("chan", "space", None)),
        out_specs=(P("chan", "space", None), P("chan", "space", None), P(None, None, "chan", None)),
        check_vma=False,
    )
```

```python
import functools

import jax
import jax.numpy as jnp
from jax import lax
from jax.experimental import pallas as pl
from jax.experimental.pallas import tpu as pltpu
from jax.sharding import PartitionSpec as P

BF = jnp.bfloat16
F32 = jnp.float32
MESH = pl.DeviceIdType.MESH
CHUNKS = 2


def shifted(value, by):
    width = value.shape[1]
    col = lax.broadcasted_iota(jnp.int32, value.shape, 1)
    edge = width - 1 if by == 1 else 0
    return jnp.where(col == edge, 0.0, pltpu.roll(value, (-by) % width, 1))


def kernel(
    n, S, x_ref, ct_ref, w_ref, act_ref, ig_ref, wg_ref,
    wb_ref, wt_ref, frame, acc, grads, sbuf, rbuf, part, pair_buf, chip_buf,
    own_sem, gs_sem, gr_sem, hs_sem, hr_sem, es_sem, er_sem, rs_sem, rr_sem,
    ps_sem, pr_sem, cs_sem, cr_sem, as_sem, ar_sem, fs_sem, fr_sem,
):
    R, Cb, W = x_ref.shape
    O = ct_ref.shape[1]
    T = 3 * O
    G = S // 2
    half = R // CHUNKS
    s = lax.axis_index("space")
    c = lax.axis_index("chan")

    barrier = pltpu.get_barrier_semaphore()
    for k in range(1, S):
        pl.semaphore_signal(barrier, 1, device_id=(lax.rem(s + k, S), c), device_id_type=MESH)

    @pl.when(c > 0)
    def _():
        pl.semaphore_signal(barrier, 1, device_id=(s, c - 1), device_id_type=MESH)

    @pl.when(c < n - 1)
    def _():
        pl.semaphore_signal(barrier, 1, device_id=(s, c + 1), device_id_type=MESH)

    own = pltpu.make_async_copy(x_ref, frame.at[c, pl.ds(1, R)], own_sem)
    own.start()
    zero_row = jnp.zeros((Cb, W), BF)

    @pl.when(s == 0)
    def _():
        for j in range(n):
            frame[j, 0] = zero_row
        grads[0] = jnp.zeros((T, W), BF)

    @pl.when(s == S - 1)
    def _():
        for j in range(n):
            frame[j, R + 1] = zero_row
        grads[R + 1] = jnp.zeros((T, W), BF)

    acc[...] = jnp.zeros_like(acc)
    pl.semaphore_wait(barrier, S - 1 + jnp.minimum(c, 1) + jnp.minimum(n - 1 - c, 1))
    own.wait()

    def peer(way):
        return (s, c + 1) if way == 0 else (s, c - 1)

    def gather_copy(way, step, part_no, block):
        rows = pl.ds(1 + part_no * half, half)
        return pltpu.make_async_remote_copy(
            src_ref=frame.at[block, rows], dst_ref=frame.at[block, rows],
            send_sem=gs_sem.at[way, step, part_no], recv_sem=gr_sem.at[way, step, part_no],
            device_id=peer(way), device_id_type=MESH,
        )

    def sends(way, step):
        if way == 0:
            return c - step, jnp.logical_and(c - step >= 0, c < n - 1)
        return c + step, jnp.logical_and(c + step <= n - 1, c > 0)

    def receives(way, step):
        if way == 0:
            return c - 1 - step, c - 1 - step >= 0
        return c + 1 + step, c + 1 + step <= n - 1

    def halo_copy(slot, side, block):
        src, dst, to = (R, 0, s + 1) if side == 0 else (1, R + 1, s - 1)
        return pltpu.make_async_remote_copy(
            src_ref=frame.at[block, src], dst_ref=frame.at[block, dst],
            send_sem=hs_sem.at[slot, side], recv_sem=hr_sem.at[slot, side],
            device_id=(to, c), device_id_type=MESH,
        )

    def halo_start(slot, block):
        @pl.when(s < S - 1)
        def _():
            halo_copy(slot, 0, block).start()

        @pl.when(s > 0)
        def _():
            halo_copy(slot, 1, block).start()

    def halo_wait(slot, block):
        @pl.when(s < S - 1)
        def _():
            halo_copy(slot, 0, block).wait_send()
            halo_copy(slot, 1, block).wait_recv()

        @pl.when(s > 0)
        def _():
            halo_copy(slot, 1, block).wait_send()
            halo_copy(slot, 0, block).wait_recv()

    def forward(block):
        def row(h, carry):
            total = acc[h]
            for a in range(3):
                total = total + jnp.dot(wb_ref[block, a], frame[block, h + a], preferred_element_type=F32)
            acc[h] = total
            return carry

        lax.fori_loop(0, R, row, 0)

    def start_gather(step, part_no):
        for way in range(2):
            block, valid = sends(way, step)

            @pl.when(valid)
            def _():
                gather_copy(way, step, part_no, block).start()

    for p in range(CHUNKS):
        start_gather(0, p)
    halo_start(0, c)

    def cut(a, carry):
        for b in range(3):
            whole = w_ref[3 * a + b]
            for j in range(n):
                wb_ref[j, a, b * O : (b + 1) * O] = whole[:, j * Cb : (j + 1) * Cb]
        return carry

    lax.fori_loop(0, 3, cut, 0)
    halo_wait(0, c)
    forward(c)

    def turn(k, carry):
        j, a = lax.div(k, 3), lax.rem(k, 3)
        wt_ref[j, a] = wb_ref[j, a].T
        return carry

    lax.fori_loop(0, 3 * n, turn, 0)
    for step in range(n - 1):
        for p in range(CHUNKS):
            for way in range(2):
                block, valid = receives(way, step)

                @pl.when(valid)
                def _():
                    gather_copy(way, step, p, block).wait_recv()

            if step < n - 2:
                start_gather(step + 1, p)
        for way in range(2):
            block, valid = receives(way, step)

            @pl.when(valid)
            def _():
                halo_start(1 + 2 * step + way, block)
        for way in range(2):
            block, valid = receives(way, step)

            @pl.when(valid)
            def _():
                halo_wait(1 + 2 * step + way, block)
                forward(block)

    def activate(h):
        pre = shifted(acc[h, :O], -1) + acc[h, O : 2 * O] + shifted(acc[h, 2 * O :], 1)
        sigma = jax.nn.sigmoid(pre)
        act_ref[h] = (pre * sigma).astype(BF)
        grad = (ct_ref[h].astype(F32) * sigma * (1.0 + pre * (1.0 - sigma))).astype(BF)
        wide = grad.astype(F32)
        grads[h + 1, :O] = shifted(wide, 1).astype(BF)
        grads[h + 1, O : 2 * O] = grad
        grads[h + 1, 2 * O :] = shifted(wide, -1).astype(BF)

    def edge_copy(side):
        src, dst, to = (R, 0, s + 1) if side == 0 else (1, R + 1, s - 1)
        return pltpu.make_async_remote_copy(
            src_ref=grads.at[src], dst_ref=grads.at[dst],
            send_sem=es_sem.at[side], recv_sem=er_sem.at[side],
            device_id=(to, c), device_id_type=MESH,
        )

    def edges(k, carry):
        activate(k * (R - 1))
        return carry

    lax.fori_loop(0, 2, edges, 0)

    @pl.when(s < S - 1)
    def _():
        edge_copy(0).start()

    @pl.when(s > 0)
    def _():
        edge_copy(1).start()

    def middle(h, carry):
        activate(h)
        return carry

    lax.fori_loop(1, R - 1, middle, 0)

    @pl.when(s < S - 1)
    def _():
        edge_copy(0).wait_send()
        edge_copy(1).wait_recv()

    @pl.when(s > 0)
    def _():
        edge_copy(1).wait_send()
        edge_copy(0).wait_recv()

    def own_row(block, h):
        total = jnp.dot(wt_ref[block, 0], grads[h + 2], preferred_element_type=F32)
        total = total + jnp.dot(wt_ref[block, 1], grads[h + 1], preferred_element_type=F32)
        return total + jnp.dot(wt_ref[block, 2], grads[h], preferred_element_type=F32)

    def scatter_dest(way, step):
        far = n - 1 - step
        if way == 0:
            return c + far, c + far <= n - 1
        return c - far, c - far >= 0

    def scatter_arrives(way, step):
        far = n - 1 - step
        if way == 0:
            return jnp.logical_and(c >= 1, c - 1 + far <= n - 1)
        return jnp.logical_and(c <= n - 2, c + 1 - far >= 0)

    def scatter_copy(way, step, part_no):
        rows = pl.ds(part_no * half, half)
        return pltpu.make_async_remote_copy(
            src_ref=sbuf.at[way, step, rows], dst_ref=rbuf.at[way, step, rows],
            send_sem=rs_sem.at[way, step, part_no], recv_sem=rr_sem.at[way, step, part_no],
            device_id=peer(way), device_id_type=MESH,
        )

    def scatter_own(step, part_no):
        for way in range(2):
            dest, valid = scatter_dest(way, step)

            @pl.when(valid)
            def _():
                def row(h, carry):
                    sbuf[way, step, h] = own_row(dest, h).astype(BF)
                    return carry

                lax.fori_loop(part_no * half, (part_no + 1) * half, row, 0)

    def scatter_send(step, part_no):
        for way in range(2):
            _, valid = scatter_dest(way, step)
            if step > 0:
                arrived = scatter_arrives(way, step - 1)

                @pl.when(arrived)
                def _():
                    scatter_copy(way, step - 1, part_no).wait_recv()

                    def row(h, carry):
                        total = sbuf[way, step, h].astype(F32) + rbuf[way, step - 1, h].astype(F32)
                        sbuf[way, step, h] = total.astype(BF)
                        return carry

                    lax.fori_loop(part_no * half, (part_no + 1) * half, row, 0)

            @pl.when(valid)
            def _():
                scatter_copy(way, step, part_no).start()

    taps = 9 * O
    lanes = n * Cb // 128

    def wgrad(k, carry):
        a, b = lax.div(k, 3), lax.rem(k, 3)
        total = jnp.zeros((O, n * Cb), F32)
        for h in range(R):
            rows = jnp.concatenate([frame[j, h + a] for j in range(n)], axis=0)
            total = total + lax.dot_general(
                grads[h + 1, pl.ds(pl.multiple_of(b * O, 16), O)], rows, (((1,), (1,)), ((), ())),
                preferred_element_type=F32,
            )
        for q in range(lanes):
            start = pl.multiple_of(q * taps + k * O, 16)
            part[pl.ds(start, O)] = total[:, q * 128 : (q + 1) * 128].astype(BF)
        return carry

    if part.shape[0] > lanes * taps:
        part[lanes * taps :] = jnp.zeros((part.shape[0] - lanes * taps, 128), BF)

    rows_all = part.shape[0]
    rows_half = rows_all // 2
    piece = rows_half // G
    side = lax.rem(s, 2)
    chip = lax.div(s, 2)
    mate = (s + 1 - 2 * side, c)
    mine = side * rows_half
    theirs = (1 - side) * rows_half

    def span(start, size):
        return pl.ds(pl.multiple_of(start, 16), size)

    def pair_copy():
        return pltpu.make_async_remote_copy(
            src_ref=part.at[span(theirs, rows_half)], dst_ref=pair_buf,
            send_sem=ps_sem, recv_sem=pr_sem, device_id=mate, device_id_type=MESH,
        )

    def chip_copy(k):
        to = lax.rem(chip + k, G)
        return pltpu.make_async_remote_copy(
            src_ref=part.at[span(mine + to * piece, piece)], dst_ref=chip_buf.at[k - 1],
            send_sem=cs_sem.at[k - 1], recv_sem=cr_sem.at[k - 1],
            device_id=(2 * to + side, c), device_id_type=MESH,
        )

    def share_copy(k):
        to = lax.rem(chip + k, G)
        rows = span(mine + chip * piece, piece)
        return pltpu.make_async_remote_copy(
            src_ref=wg_ref.at[rows], dst_ref=wg_ref.at[rows],
            send_sem=as_sem.at[k - 1], recv_sem=ar_sem.at[k - 1],
            device_id=(2 * to + side, c), device_id_type=MESH,
        )

    def mate_copy(k):
        origin = lax.rem(chip - k + G, G)
        rows = span(mine + origin * piece, piece)
        return pltpu.make_async_remote_copy(
            src_ref=wg_ref.at[rows], dst_ref=wg_ref.at[rows],
            send_sem=fs_sem.at[k], recv_sem=fr_sem.at[k],
            device_id=mate, device_id_type=MESH,
        )

    def reduce_stage(stage):
        if stage == 0:
            pair_copy().start()
        elif stage == 1:
            pair_copy().wait()

            def add(i, carry):
                rows = span(mine + i * piece, piece)
                got = pair_buf[span(i * piece, piece)].astype(F32)
                part[rows] = (part[rows].astype(F32) + got).astype(BF)
                return carry

            lax.fori_loop(0, G, add, 0)
            for k in range(1, G):
                chip_copy(k).start()
        elif stage == 2:
            for k in range(1, G):
                chip_copy(k).wait()

            rows = span(mine + chip * piece, piece)
            total = part[rows].astype(F32)
            for k in range(1, G):
                total = total + chip_buf[k - 1].astype(F32)
            wg_ref[rows] = total.astype(BF)
            for k in range(1, G):
                share_copy(k).start()
            mate_copy(0).start()
        else:
            for k in range(1, G):
                share_copy(k).wait()
                mate_copy(k).start()

    for p in range(CHUNKS):
        scatter_own(0, p)
        scatter_send(0, p)

    lax.fori_loop(0, 9, wgrad, 0)
    reduce_stage(0)
    stage = 1
    for step in range(1, n - 1):
        for p in range(CHUNKS):
            scatter_own(step, p)
        if stage == 1:
            reduce_stage(stage)
            stage += 1
        for p in range(CHUNKS):
            scatter_send(step, p)
        if step == 2:
            reduce_stage(stage)
            stage += 1

    def row(h, carry):
        acc[h, :Cb] = own_row(c, h)
        return carry

    lax.fori_loop(0, R, row, 0)
    while stage < 4:
        reduce_stage(stage)
        stage += 1

    for way in range(2):
        arrived = scatter_arrives(way, n - 2)

        @pl.when(arrived)
        def _():
            for p in range(CHUNKS):
                scatter_copy(way, n - 2, p).wait_recv()

            def row(h, carry):
                acc[h, :Cb] = acc[h, :Cb] + rbuf[way, n - 2, h].astype(F32)
                return carry

            lax.fori_loop(0, R, row, 0)

    def last(h, carry):
        ig_ref[h] = acc[h, :Cb].astype(BF)
        return carry

    lax.fori_loop(0, R, last, 0)

    for k in range(G):
        mate_copy(k).wait()
    for step in range(n - 1):
        for way in range(2):
            block, valid = sends(way, step)
            _, out = scatter_dest(way, step)

            @pl.when(valid)
            def _():
                for p in range(CHUNKS):
                    gather_copy(way, step, p, block).wait_send()

            @pl.when(out)
            def _():
                for p in range(CHUNKS):
                    scatter_copy(way, step, p).wait_send()


def widen_kernel(in_ref, out_ref):
    for q in range(in_ref.shape[0]):
        out_ref[:, q * 128 : (q + 1) * 128] = in_ref[q].astype(F32)


def on_device(n, S, images, weight, cotangent):
    Cb, R, W = images.shape
    O = weight.shape[2]
    T = 3 * O
    x = images.transpose(1, 0, 2)
    ct = cotangent.transpose(1, 0, 2)
    w = weight.reshape(9, O, n * Cb)
    lanes = n * Cb // 128
    rows = lanes * 9 * O
    rows_all = -(-rows // (16 * S)) * 16 * S
    dma = pltpu.SemaphoreType.DMA
    vmem = pl.BlockSpec(memory_space=pltpu.VMEM)
    act, ig, wg = pl.pallas_call(
        functools.partial(kernel, n, S),
        out_shape=(
            jax.ShapeDtypeStruct((R, O, W), BF),
            jax.ShapeDtypeStruct((R, Cb, W), BF),
            jax.ShapeDtypeStruct((rows_all, 128), BF),
        ),
        in_specs=[vmem] * 3,
        out_specs=(vmem, vmem, vmem),
        scratch_shapes=[
            pltpu.VMEM((n, 3, T, Cb), BF),
            pltpu.VMEM((n, 3, Cb, T), BF),
            pltpu.VMEM((n, R + 2, Cb, W), BF),
            pltpu.VMEM((R, T, W), F32),
            pltpu.VMEM((R + 2, T, W), BF),
            pltpu.VMEM((2, n - 1, R, Cb, W), BF),
            pltpu.VMEM((2, n - 1, R, Cb, W), BF),
            pltpu.VMEM((rows_all, 128), BF),
            pltpu.VMEM((rows_all // 2, 128), BF),
            pltpu.VMEM((S // 2 - 1, rows_all // S, 128), BF),
            dma,
            dma((2, n - 1, CHUNKS)), dma((2, n - 1, CHUNKS)),
            dma((2 * n - 1, 2)), dma((2 * n - 1, 2)),
            dma((2,)), dma((2,)),
            dma((2, n - 1, CHUNKS)), dma((2, n - 1, CHUNKS)),
            dma, dma,
            dma((S // 2 - 1,)), dma((S // 2 - 1,)),
            dma((S // 2 - 1,)), dma((S // 2 - 1,)),
            dma((S // 2,)), dma((S // 2,)),
        ],
        compiler_params=pltpu.CompilerParams(
            collective_id=0, has_side_effects=True, vmem_limit_bytes=60 * 2**20
        ),
    )(x, ct, w)
    wg = wg[:rows].reshape(lanes, 9 * O, 128)
    weight_grad = pl.pallas_call(
        widen_kernel,
        grid=(9,),
        in_specs=[pl.BlockSpec((lanes, O, 128), lambda k: (0, k, 0))],
        out_specs=pl.BlockSpec((O, n * Cb), lambda k: (k, 0)),
        out_shape=jax.ShapeDtypeStruct((9 * O, n * Cb), F32),
    )(wg)
    return (
        act.transpose(1, 0, 2),
        ig.transpose(1, 0, 2),
        weight_grad.reshape(3, 3, O, n * Cb),
    )


def solution(mesh):
    return jax.shard_map(
        functools.partial(on_device, mesh.shape["chan"], mesh.shape["space"]),
        mesh=mesh,
        in_specs=(P("chan", "space", None), P(None, None, "chan", None), P("chan", "space", None)),
        out_specs=(P("chan", "space", None), P("chan", "space", None), P(None, None, "chan", None)),
        check_vma=False,
    )
```

```python
import functools

import jax
import jax.numpy as jnp
from jax import lax
from jax.experimental import pallas as pl
from jax.experimental.pallas import tpu as pltpu
from jax.sharding import PartitionSpec as P

BF = jnp.bfloat16
F32 = jnp.float32
MESH = pl.DeviceIdType.MESH
CHUNKS = 2


def shifted(value, by):
    width = value.shape[1]
    col = lax.broadcasted_iota(jnp.int32, value.shape, 1)
    edge = width - 1 if by == 1 else 0
    return jnp.where(col == edge, 0.0, pltpu.roll(value, (-by) % width, 1))


def kernel(
    n, S, x_ref, ct_ref, w_ref, act_ref, ig_ref, wg_ref,
    wb_ref, wt_ref, frame, acc, grads, sbuf, rbuf, part, pair_buf, chip_buf,
    own_sem, gs_sem, gr_sem, hs_sem, hr_sem, es_sem, er_sem, rs_sem, rr_sem,
    ps_sem, pr_sem, cs_sem, cr_sem, as_sem, ar_sem, fs_sem, fr_sem,
):
    R, Cb, W = x_ref.shape
    O = ct_ref.shape[1]
    T = 3 * O
    G = S // 2
    half = R // CHUNKS
    s = lax.axis_index("space")
    c = lax.axis_index("chan")

    barrier = pltpu.get_barrier_semaphore()
    for k in range(1, S):
        pl.semaphore_signal(barrier, 1, device_id=(lax.rem(s + k, S), c), device_id_type=MESH)

    @pl.when(c > 0)
    def _():
        pl.semaphore_signal(barrier, 1, device_id=(s, c - 1), device_id_type=MESH)

    @pl.when(c < n - 1)
    def _():
        pl.semaphore_signal(barrier, 1, device_id=(s, c + 1), device_id_type=MESH)

    own = pltpu.make_async_copy(x_ref, frame.at[c, pl.ds(1, R)], own_sem)
    own.start()
    zero_row = jnp.zeros((Cb, W), BF)

    @pl.when(s == 0)
    def _():
        for j in range(n):
            frame[j, 0] = zero_row
        grads[0] = jnp.zeros((T, W), BF)

    @pl.when(s == S - 1)
    def _():
        for j in range(n):
            frame[j, R + 1] = zero_row
        grads[R + 1] = jnp.zeros((T, W), BF)

    acc[...] = jnp.zeros_like(acc)
    pl.semaphore_wait(barrier, S - 1 + jnp.minimum(c, 1) + jnp.minimum(n - 1 - c, 1))
    own.wait()

    def peer(way):
        return (s, c + 1) if way == 0 else (s, c - 1)

    def gather_copy(way, step, part_no, block):
        rows = pl.ds(1 + part_no * half, half)
        return pltpu.make_async_remote_copy(
            src_ref=frame.at[block, rows], dst_ref=frame.at[block, rows],
            send_sem=gs_sem.at[way, step, part_no], recv_sem=gr_sem.at[way, step, part_no],
            device_id=peer(way), device_id_type=MESH,
        )

    def sends(way, step):
        if way == 0:
            return c - step, jnp.logical_and(c - step >= 0, c < n - 1)
        return c + step, jnp.logical_and(c + step <= n - 1, c > 0)

    def receives(way, step):
        if way == 0:
            return c - 1 - step, c - 1 - step >= 0
        return c + 1 + step, c + 1 + step <= n - 1

    def halo_copy(slot, side, block):
        src, dst, to = (R, 0, s + 1) if side == 0 else (1, R + 1, s - 1)
        return pltpu.make_async_remote_copy(
            src_ref=frame.at[block, src], dst_ref=frame.at[block, dst],
            send_sem=hs_sem.at[slot, side], recv_sem=hr_sem.at[slot, side],
            device_id=(to, c), device_id_type=MESH,
        )

    def halo_start(slot, block):
        @pl.when(s < S - 1)
        def _():
            halo_copy(slot, 0, block).start()

        @pl.when(s > 0)
        def _():
            halo_copy(slot, 1, block).start()

    def halo_wait(slot, block):
        @pl.when(s < S - 1)
        def _():
            halo_copy(slot, 0, block).wait_send()
            halo_copy(slot, 1, block).wait_recv()

        @pl.when(s > 0)
        def _():
            halo_copy(slot, 1, block).wait_send()
            halo_copy(slot, 0, block).wait_recv()

    def forward(block):
        def row(h, carry):
            total = acc[h]
            for a in range(3):
                total = total + jnp.dot(wb_ref[block, a], frame[block, h + a], preferred_element_type=F32)
            acc[h] = total
            return carry

        lax.fori_loop(0, R, row, 0)

    def start_gather(step, part_no):
        for way in range(2):
            block, valid = sends(way, step)

            @pl.when(valid)
            def _():
                gather_copy(way, step, part_no, block).start()

    for p in range(CHUNKS):
        start_gather(0, p)
    halo_start(0, c)

    def cut(a, carry):
        for b in range(3):
            whole = w_ref[3 * a + b]
            for j in range(n):
                wb_ref[j, a, b * O : (b + 1) * O] = whole[:, j * Cb : (j + 1) * Cb]
        return carry

    lax.fori_loop(0, 3, cut, 0)
    halo_wait(0, c)
    forward(c)

    def turn(k, carry):
        j, a = lax.div(k, 3), lax.rem(k, 3)
        wt_ref[j, a] = wb_ref[j, a].T
        return carry

    lax.fori_loop(0, 3 * n, turn, 0)
    for step in range(n - 1):
        for p in range(CHUNKS):
            for way in range(2):
                block, valid = receives(way, step)

                @pl.when(valid)
                def _():
                    gather_copy(way, step, p, block).wait_recv()

                if step < n - 2:
                    onward, more = sends(way, step + 1)

                    @pl.when(more)
                    def _():
                        gather_copy(way, step + 1, p, onward).start()

        for way in range(2):
            block, valid = receives(way, step)

            @pl.when(valid)
            def _():
                halo_start(1 + 2 * step + way, block)
        for way in range(2):
            block, valid = receives(way, step)

            @pl.when(valid)
            def _():
                halo_wait(1 + 2 * step + way, block)
                forward(block)

    def activate(h):
        pre = shifted(acc[h, :O], -1) + acc[h, O : 2 * O] + shifted(acc[h, 2 * O :], 1)
        sigma = jax.nn.sigmoid(pre)
        act_ref[h] = (pre * sigma).astype(BF)
        grad = (ct_ref[h].astype(F32) * sigma * (1.0 + pre * (1.0 - sigma))).astype(BF)
        wide = grad.astype(F32)
        grads[h + 1, :O] = shifted(wide, 1).astype(BF)
        grads[h + 1, O : 2 * O] = grad
        grads[h + 1, 2 * O :] = shifted(wide, -1).astype(BF)

    def edge_copy(side):
        src, dst, to = (R, 0, s + 1) if side == 0 else (1, R + 1, s - 1)
        return pltpu.make_async_remote_copy(
            src_ref=grads.at[src], dst_ref=grads.at[dst],
            send_sem=es_sem.at[side], recv_sem=er_sem.at[side],
            device_id=(to, c), device_id_type=MESH,
        )

    def edges(k, carry):
        activate(k * (R - 1))
        return carry

    lax.fori_loop(0, 2, edges, 0)

    @pl.when(s < S - 1)
    def _():
        edge_copy(0).start()

    @pl.when(s > 0)
    def _():
        edge_copy(1).start()

    def middle(h, carry):
        activate(h)
        return carry

    lax.fori_loop(1, R - 1, middle, 0)

    @pl.when(s < S - 1)
    def _():
        edge_copy(0).wait_send()
        edge_copy(1).wait_recv()

    @pl.when(s > 0)
    def _():
        edge_copy(1).wait_send()
        edge_copy(0).wait_recv()

    def own_row(block, h):
        total = jnp.dot(wt_ref[block, 0], grads[h + 2], preferred_element_type=F32)
        total = total + jnp.dot(wt_ref[block, 1], grads[h + 1], preferred_element_type=F32)
        return total + jnp.dot(wt_ref[block, 2], grads[h], preferred_element_type=F32)

    def scatter_dest(way, step):
        far = n - 1 - step
        if way == 0:
            return c + far, c + far <= n - 1
        return c - far, c - far >= 0

    def scatter_arrives(way, step):
        far = n - 1 - step
        if way == 0:
            return jnp.logical_and(c >= 1, c - 1 + far <= n - 1)
        return jnp.logical_and(c <= n - 2, c + 1 - far >= 0)

    def scatter_copy(way, step, part_no):
        rows = pl.ds(part_no * half, half)
        return pltpu.make_async_remote_copy(
            src_ref=sbuf.at[way, step, rows], dst_ref=rbuf.at[way, step, rows],
            send_sem=rs_sem.at[way, step, part_no], recv_sem=rr_sem.at[way, step, part_no],
            device_id=peer(way), device_id_type=MESH,
        )

    def scatter_own(step, part_no):
        for way in range(2):
            dest, valid = scatter_dest(way, step)

            @pl.when(valid)
            def _():
                def row(h, carry):
                    sbuf[way, step, h] = own_row(dest, h).astype(BF)
                    return carry

                lax.fori_loop(part_no * half, (part_no + 1) * half, row, 0)

    def scatter_send(step, part_no):
        for way in range(2):
            _, valid = scatter_dest(way, step)
            if step > 0:
                arrived = scatter_arrives(way, step - 1)

                @pl.when(arrived)
                def _():
                    scatter_copy(way, step - 1, part_no).wait_recv()

                    def row(h, carry):
                        total = sbuf[way, step, h].astype(F32) + rbuf[way, step - 1, h].astype(F32)
                        sbuf[way, step, h] = total.astype(BF)
                        return carry

                    lax.fori_loop(part_no * half, (part_no + 1) * half, row, 0)

            @pl.when(valid)
            def _():
                scatter_copy(way, step, part_no).start()

    taps = 9 * O
    lanes = n * Cb // 128

    def wgrad(k, carry):
        a, b = lax.div(k, 3), lax.rem(k, 3)
        total = jnp.zeros((O, n * Cb), F32)
        for h in range(R):
            rows = jnp.concatenate([frame[j, h + a] for j in range(n)], axis=0)
            total = total + lax.dot_general(
                grads[h + 1, pl.ds(pl.multiple_of(b * O, 16), O)], rows, (((1,), (1,)), ((), ())),
                preferred_element_type=F32,
            )
        for q in range(lanes):
            start = pl.multiple_of(q * taps + k * O, 16)
            part[pl.ds(start, O)] = total[:, q * 128 : (q + 1) * 128].astype(BF)
        return carry

    if part.shape[0] > lanes * taps:
        part[lanes * taps :] = jnp.zeros((part.shape[0] - lanes * taps, 128), BF)

    rows_all = part.shape[0]
    rows_half = rows_all // 2
    piece = rows_half // G
    side = lax.rem(s, 2)
    chip = lax.div(s, 2)
    mate = (s + 1 - 2 * side, c)
    mine = side * rows_half
    theirs = (1 - side) * rows_half

    def span(start, size):
        return pl.ds(pl.multiple_of(start, 16), size)

    def pair_copy():
        return pltpu.make_async_remote_copy(
            src_ref=part.at[span(theirs, rows_half)], dst_ref=pair_buf,
            send_sem=ps_sem, recv_sem=pr_sem, device_id=mate, device_id_type=MESH,
        )

    def chip_copy(k):
        to = lax.rem(chip + k, G)
        return pltpu.make_async_remote_copy(
            src_ref=part.at[span(mine + to * piece, piece)], dst_ref=chip_buf.at[k - 1],
            send_sem=cs_sem.at[k - 1], recv_sem=cr_sem.at[k - 1],
            device_id=(2 * to + side, c), device_id_type=MESH,
        )

    def share_copy(k):
        to = lax.rem(chip + k, G)
        rows = span(mine + chip * piece, piece)
        return pltpu.make_async_remote_copy(
            src_ref=wg_ref.at[rows], dst_ref=wg_ref.at[rows],
            send_sem=as_sem.at[k - 1], recv_sem=ar_sem.at[k - 1],
            device_id=(2 * to + side, c), device_id_type=MESH,
        )

    def mate_copy(k):
        origin = lax.rem(chip - k + G, G)
        rows = span(mine + origin * piece, piece)
        return pltpu.make_async_remote_copy(
            src_ref=wg_ref.at[rows], dst_ref=wg_ref.at[rows],
            send_sem=fs_sem.at[k], recv_sem=fr_sem.at[k],
            device_id=mate, device_id_type=MESH,
        )

    def reduce_stage(stage):
        if stage == 0:
            pair_copy().start()
        elif stage == 1:
            pair_copy().wait()

            def add(i, carry):
                rows = span(mine + i * piece, piece)
                got = pair_buf[span(i * piece, piece)].astype(F32)
                part[rows] = (part[rows].astype(F32) + got).astype(BF)
                return carry

            lax.fori_loop(0, G, add, 0)
            for k in range(1, G):
                chip_copy(k).start()
        elif stage == 2:
            for k in range(1, G):
                chip_copy(k).wait()

            rows = span(mine + chip * piece, piece)
            total = part[rows].astype(F32)
            for k in range(1, G):
                total = total + chip_buf[k - 1].astype(F32)
            wg_ref[rows] = total.astype(BF)
            for k in range(1, G):
                share_copy(k).start()
            mate_copy(0).start()
        else:
            for k in range(1, G):
                share_copy(k).wait()
                mate_copy(k).start()

    for p in range(CHUNKS):
        scatter_own(0, p)
        scatter_send(0, p)

    lax.fori_loop(0, 9, wgrad, 0)
    reduce_stage(0)
    stage = 1
    for step in range(1, n - 1):
        for p in range(CHUNKS):
            scatter_own(step, p)
        if stage == 1:
            reduce_stage(stage)
            stage += 1
        for p in range(CHUNKS):
            scatter_send(step, p)
        if step == 2:
            reduce_stage(stage)
            stage += 1

    def row(h, carry):
        acc[h, :Cb] = own_row(c, h)
        return carry

    lax.fori_loop(0, R, row, 0)
    while stage < 4:
        reduce_stage(stage)
        stage += 1

    for way in range(2):
        arrived = scatter_arrives(way, n - 2)

        @pl.when(arrived)
        def _():
            for p in range(CHUNKS):
                scatter_copy(way, n - 2, p).wait_recv()

            def row(h, carry):
                acc[h, :Cb] = acc[h, :Cb] + rbuf[way, n - 2, h].astype(F32)
                return carry

            lax.fori_loop(0, R, row, 0)

    def last(h, carry):
        ig_ref[h] = acc[h, :Cb].astype(BF)
        return carry

    lax.fori_loop(0, R, last, 0)

    for k in range(G):
        mate_copy(k).wait()
    for step in range(n - 1):
        for way in range(2):
            block, valid = sends(way, step)
            _, out = scatter_dest(way, step)

            @pl.when(valid)
            def _():
                for p in range(CHUNKS):
                    gather_copy(way, step, p, block).wait_send()

            @pl.when(out)
            def _():
                for p in range(CHUNKS):
                    scatter_copy(way, step, p).wait_send()


def widen_kernel(in_ref, out_ref):
    for q in range(in_ref.shape[0]):
        out_ref[:, q * 128 : (q + 1) * 128] = in_ref[q].astype(F32)


def on_device(n, S, images, weight, cotangent):
    Cb, R, W = images.shape
    O = weight.shape[2]
    T = 3 * O
    x = images.transpose(1, 0, 2)
    ct = cotangent.transpose(1, 0, 2)
    w = weight.reshape(9, O, n * Cb)
    lanes = n * Cb // 128
    rows = lanes * 9 * O
    rows_all = -(-rows // (16 * S)) * 16 * S
    dma = pltpu.SemaphoreType.DMA
    vmem = pl.BlockSpec(memory_space=pltpu.VMEM)
    act, ig, wg = pl.pallas_call(
        functools.partial(kernel, n, S),
        out_shape=(
            jax.ShapeDtypeStruct((R, O, W), BF),
            jax.ShapeDtypeStruct((R, Cb, W), BF),
            jax.ShapeDtypeStruct((rows_all, 128), BF),
        ),
        in_specs=[vmem] * 3,
        out_specs=(vmem, vmem, vmem),
        scratch_shapes=[
            pltpu.VMEM((n, 3, T, Cb), BF),
            pltpu.VMEM((n, 3, Cb, T), BF),
            pltpu.VMEM((n, R + 2, Cb, W), BF),
            pltpu.VMEM((R, T, W), F32),
            pltpu.VMEM((R + 2, T, W), BF),
            pltpu.VMEM((2, n - 1, R, Cb, W), BF),
            pltpu.VMEM((2, n - 1, R, Cb, W), BF),
            pltpu.VMEM((rows_all, 128), BF),
            pltpu.VMEM((rows_all // 2, 128), BF),
            pltpu.VMEM((S // 2 - 1, rows_all // S, 128), BF),
            dma,
            dma((2, n - 1, CHUNKS)), dma((2, n - 1, CHUNKS)),
            dma((2 * n - 1, 2)), dma((2 * n - 1, 2)),
            dma((2,)), dma((2,)),
            dma((2, n - 1, CHUNKS)), dma((2, n - 1, CHUNKS)),
            dma, dma,
            dma((S // 2 - 1,)), dma((S // 2 - 1,)),
            dma((S // 2 - 1,)), dma((S // 2 - 1,)),
            dma((S // 2,)), dma((S // 2,)),
        ],
        compiler_params=pltpu.CompilerParams(
            collective_id=0, has_side_effects=True, vmem_limit_bytes=60 * 2**20
        ),
    )(x, ct, w)
    wg = wg[:rows].reshape(lanes, 9 * O, 128)
    weight_grad = pl.pallas_call(
        widen_kernel,
        grid=(3,),
        in_specs=[pl.BlockSpec((lanes, T, 128), lambda k: (0, k, 0))],
        out_specs=pl.BlockSpec((T, n * Cb), lambda k: (k, 0)),
        out_shape=jax.ShapeDtypeStruct((9 * O, n * Cb), F32),
    )(wg)
    return (
        act.transpose(1, 0, 2),
        ig.transpose(1, 0, 2),
        weight_grad.reshape(3, 3, O, n * Cb),
    )


def solution(mesh):
    return jax.shard_map(
        functools.partial(on_device, mesh.shape["chan"], mesh.shape["space"]),
        mesh=mesh,
        in_specs=(P("chan", "space", None), P(None, None, "chan", None), P("chan", "space", None)),
        out_specs=(P("chan", "space", None), P("chan", "space", None), P(None, None, "chan", None)),
        check_vma=False,
    )
```
